256 devices in a mesh: occ: 8 (over x, y_hi), vir: 32 (over z, y_lo, core).
Axes of the slice: x: 4, y: 4 (y_hi: 2, y_lo: 2; y = y_hi * 2 + y_lo), z: 8, core: 2. Of those that a mesh axis runs over, the one named last changes fastest.
Arguments:
- amplitudes: bfloat16 [6144, 65536], P('occ', 'vir'), may hold values from -6 to 6
- integrals: bfloat16 [65536, 4096], P('vir', 'occ'), may hold values from -0.046875 to 0.046875
- other_terms: float32 [6144, 4096], P('occ', 'vir'), may hold values from -6 to 6
- occ_pairs: int32 [2, 6144], P(None, 'occ'), may hold values from 0 to 199
- vir_a: int32 [16], replicated, may hold values from 0 to 1999
- vir_b: int32 [256], replicated, may hold values from 0 to 1999
- eps_occ: float32 [200], replicated, may hold values from -3 to -0.3
- eps_vir: float32 [2000], replicated, may hold values from 0.2 to 3
Outputs:
- new_amplitudes: float32 [6144, 4096], P('occ', 'vir')
The draws below stay inside these ranges and needn't reach their ends.
All inputs are finite; a program needn't handle non-finite values.
Results may differ from the reference program's by a relative error of at most 0.0003.
Values may be sent and summed in bfloat16 or wider, within the bound.
No kernel may reach another device: no remote copies, remote signals or barrier semaphores. Data moves between devices by JAX's collectives and lax.ppermute only.
A program may use at most 128 MiB of HBM per device.

```python
import jax
import jax.numpy as jnp
from jax import lax

NO = 200
NV = 2000
NVIRR = 256
AWIN = 16
PAIR_DEV = 768
PAIRS = 6144
KPAIRS = 65536
ABCOLS = 4096
N_OCC = 8


def with_ends(entries, stream_key, low, top_value):
    longest = entries.shape.index(max(entries.shape))
    spots = []
    for shift in (0, 1):
        where = [jax.random.randint(jax.random.fold_in(stream_key, axis), (), 0, length) for axis, length in enumerate(entries.shape)]
        where[longest] = (where[longest] + shift) % entries.shape[longest]
        spots.append(tuple(where))
    return entries.at[spots[0]].set(low).at[spots[1]].set(top_value)


def spiked(array, key, source, target, blocks, factor):
    owner, partner = [(jnp.arange(array.shape[position]) // (array.shape[position] // blocks)).reshape([-1 if axis == position else 1 for axis in range(array.ndim)]) for position in (source, target)]
    chosen = jax.random.permutation(key, blocks)[partner]
    strong = (owner == chosen) | (owner == (partner + blocks // 2) % blocks)
    return jnp.where(strong, factor * array, array)


def block_scale(key, shape, shards, least, largest):
    def one(axis_at, parts):
        draws = jax.random.uniform(jax.random.fold_in(jax.random.fold_in(key, 6), axis_at), (parts,), jnp.float32, least / len(shards), largest / len(shards))
        return jnp.repeat(jnp.exp(draws), shape[axis_at] // parts).reshape((-1,) + (1,) * (len(shape) - axis_at - 1))

    gain = one(*shards[0])
    for cut in shards[1:]:
        gain = gain * one(*cut)
    return gain


def normal_values(rng, shape, deviation, most, cuts=(), kind=jnp.bfloat16):
    gain = block_scale(rng, shape, cuts, -0.22, 0.18) if cuts else 1.0
    array = jax.random.normal(rng, shape, jnp.float32) * deviation * gain
    return jnp.minimum(jnp.maximum(array, -most), most).astype(kind)


def gaussian_with(own_key, extent, scale, bound, pieces, heavy, kind=jnp.bfloat16):
    array = scale * jax.random.normal(own_key, extent, jnp.float32)
    if pieces:
        array = array * block_scale(own_key, extent, pieces, -0.22, 0.18)
    return jnp.clip(spiked(array, jax.random.fold_in(own_key, 3), *heavy), -bound, bound).astype(kind)


def setup_inputs(seed: int = 0) -> dict:
    keys = jax.random.split(jax.random.key(seed), 9)
    return {
        "amplitudes": normal_values(keys[0], (PAIRS, KPAIRS), 1.0, 6.0, ((0, 8), (1, 32))),
        "integrals": gaussian_with(keys[1], (KPAIRS, ABCOLS), KPAIRS ** -0.5, 0.046875, ((0, 32), (1, 8)), (0, 1, 32, 2.75)),
        "other_terms": normal_values(keys[2], (PAIRS, ABCOLS), 1.0, 6.0, ((0, 8), (1, 32)), jnp.float32),
        "occ_pairs": with_ends(jax.random.randint(keys[3], (2, PAIRS), 0, NO), jax.random.fold_in(keys[3], 1), 0, NO - 1).astype(jnp.int32),
        "vir_a": with_ends(jax.random.randint(keys[4], (AWIN,), 0, NV), jax.random.fold_in(keys[4], 1), 0, NV - 1).astype(jnp.int32),
        "vir_b": with_ends(jax.random.randint(keys[5], (NVIRR,), 0, NV), jax.random.fold_in(keys[5], 1), 0, NV - 1).astype(jnp.int32),
        "eps_occ": jnp.clip(jax.random.uniform(keys[6], (NO,), jnp.float32, -3.0, -0.3), -3.0, -0.3),
        "eps_vir": jnp.clip(jax.random.uniform(keys[7], (NV,), jnp.float32, 0.2, 3.0), 0.2, 3.0),
    }


def reference(amplitudes, integrals, other_terms, occ_pairs, vir_a, vir_b, eps_occ, eps_vir):
    blocks = amplitudes.reshape(N_OCC, PAIR_DEV, amplitudes.shape[1])

    def one_block(rows_block):
        return jnp.dot(rows_block, integrals, preferred_element_type=jnp.float32)

    ladder = lax.map(one_block, blocks).reshape(amplitudes.shape[0], integrals.shape[1])
    a_orbital = jnp.repeat(vir_a, NVIRR)
    b_orbital = jnp.tile(vir_b, AWIN)
    column_energy = eps_vir[a_orbital] + eps_vir[b_orbital]
    row_energy = eps_occ[occ_pairs[0]] + eps_occ[occ_pairs[1]]
    denominator = column_energy[None, :] - row_energy[:, None]
    return (other_terms + ladder) / denominator
```

```python
import jax
import jax.numpy as jnp
from jax import lax
from jax.sharding import PartitionSpec as P

AXES = ("occ", "vir")
NX, NYH, NZ, NYL, NC = 4, 2, 8, 2, 2
SCALE_PART = 32.0
SCALE_SUM = 4.0


def device_id(x, yh, z, yl, c):
    return ((x % NX) * NYH + yh % NYH) * (NZ * NYL * NC) + ((z % NZ) * NYL + yl % NYL) * NC + c % NC


def everywhere():
    return [
        (x, yh, z, yl, c)
        for x in range(NX)
        for yh in range(NYH)
        for z in range(NZ)
        for yl in range(NYL)
        for c in range(NC)
    ]


def moved(target):
    return [(device_id(*spot), device_id(*target(*spot))) for spot in everywhere()]


X_UP = moved(lambda x, yh, z, yl, c: (x + 1, yh, z, yl, c))
X_DOWN = moved(lambda x, yh, z, yl, c: (x - 1, yh, z, yl, c))
Y_FAR = moved(lambda x, yh, z, yl, c: (x, yh + 1, z, yl, c))
CORE = moved(lambda x, yh, z, yl, c: (x, yh, z, yl, c + 1))
HOME = moved(lambda x, yh, z, yl, c: (x, z % 2, z - z % 2 + yh, yl, c))
HOME_NEXT = moved(lambda x, yh, z, yl, c: (x, z % 2, z - z % 2 + yh, yl + 1, c))
Z_GROUPS = [
    [device_id(x, yh, 2 * ((x + j // 2) % NX) + (yh + j % 2) % NYH, yl, c) for j in range(NZ)]
    for x in range(NX)
    for yh in range(NYH)
    for yl in range(NYL)
    for c in range(NC)
]


def send(block, route):
    return lax.ppermute(block, AXES, route)


def over_z(pieces):
    return lax.all_to_all(pieces, AXES, 0, 0, axis_index_groups=Z_GROUPS, tiled=True)


def lookup(indices, table):
    positions = jnp.arange(table.shape[0], dtype=jnp.int32)
    return jnp.sum(jnp.where(indices[:, None] == positions[None, :], table[None, :], 0.0), axis=1)


def stripes(rows, cols):
    out = jnp.dot(rows, cols, preferred_element_type=jnp.float32) * SCALE_PART
    out = out.astype(jnp.float16)
    units = rows.shape[0] // 256
    return [out[256 * u : 256 * (u + 1)].reshape(NZ, 32, 256) for u in range(units)]


def reduce_z(batch):
    got = over_z(jnp.concatenate(batch, axis=1))
    total = jnp.sum(got.astype(jnp.float32), axis=0) * (SCALE_SUM / SCALE_PART)
    total = total.astype(jnp.float16)
    return [total[32 * u : 32 * (u + 1)] for u in range(len(batch))]


def per_device(amplitudes, integrals, other_terms, occ_pairs, vir_a, vir_b, eps_occ, eps_vir):
    vir = lax.axis_index("vir")
    core = vir % NC
    y_low = (vir // NC) % NYL
    barrier = lax.optimization_barrier

    def columns(which, of_core):
        return lax.dynamic_slice_in_dim(integrals, which * 256 + of_core * 128, 128, axis=1)

    b = [
        jnp.concatenate([columns(j, core), send(columns(j, 1 - core), CORE)], axis=0) for j in range(2)
    ]
    p1, m1, ay0 = send(b[0], X_UP), send(b[1], X_DOWN), send(amplitudes[:256], Y_FAR)
    own = jnp.concatenate([amplitudes, send(amplitudes, CORE)], axis=1)
    q0 = jnp.concatenate(b, axis=1)
    s0 = reduce_z(stripes(own, q0))
    p1, m1, ay0, a1 = barrier((p1, m1, ay0, amplitudes[256:512]))
    p2, m2, ay1 = send(p1, X_UP), send(m1, X_DOWN), send(a1, Y_FAR)
    far0 = jnp.concatenate([ay0, send(ay0, CORE)], axis=1)
    q1 = jnp.concatenate([p1, m1], axis=1)
    s1 = reduce_z(stripes(own, q1) + stripes(far0, q0) + stripes(far0, q1))
    p2, m2, ay1, a2, b0, b1 = barrier((p2, m2, ay1, amplitudes[512:], b[0], b[1]))
    p3, m3, ay2 = send(b1, X_UP), send(b0, X_DOWN), send(a2, Y_FAR)
    far1 = jnp.concatenate([ay1, send(ay1, CORE)], axis=1)
    q2 = jnp.concatenate([p2, m2], axis=1)
    s2 = reduce_z(
        stripes(own, q2) + stripes(far0, q2) + stripes(far1, q0) + stripes(far1, q1) + stripes(far1, q2)
    )
    far2 = jnp.concatenate([ay2, send(ay2, CORE)], axis=1)
    q3 = jnp.concatenate([p3, m3], axis=1)
    s3 = reduce_z(
        stripes(own, q3)
        + stripes(far0, q3)
        + stripes(far1, q3)
        + stripes(far2, q0)
        + stripes(far2, q1)
        + stripes(far2, q2)
        + stripes(far2, q3)
    )
    held = {}
    for u in range(3):
        for q, s in enumerate((s0, s1, s2, s3)):
            held[u, q] = s[u]
    held[3, 0], held[3, 1] = s1[3], s1[4]
    held[3, 2], held[4, 0], held[4, 1], held[4, 2] = s2[3], s2[4], s2[5], s2[6]
    held[3, 3], held[4, 3] = s3[3], s3[4]
    for q in range(4):
        held[5, q] = s3[5 + q]
    slots = []
    for shift in range(4):
        for far in range(2):
            rows = []
            for u in range(3):
                at = [held[3 * far + u, q] for q in range(4)]
                if shift == 0:
                    rows.append(at[0])
                elif shift == 1:
                    rows.append(jnp.concatenate([at[3][:, 128:], at[1][:, 128:]], axis=1))
                elif shift == 2:
                    rows.append(at[2])
                else:
                    rows.append(jnp.concatenate([at[1][:, :128], at[3][:, :128]], axis=1))
            slots.append(jnp.concatenate(rows, axis=0))
    got = over_z(jnp.stack(slots))
    got = got.reshape(NZ, 3, 32, 256).transpose(1, 0, 2, 3).reshape(768, 256)
    mine = lax.dynamic_slice_in_dim(got, y_low * 128, 128, axis=1)
    next_one = lax.dynamic_slice_in_dim(got, (1 - y_low) * 128, 128, axis=1)
    mine, next_one = send(mine, HOME), send(next_one, HOME_NEXT)
    ladder = (mine.astype(jnp.float32) + next_one.astype(jnp.float32)) * (1.0 / SCALE_SUM)

    local_cols = other_terms.shape[1]
    global_col = vir * local_cols + jnp.arange(local_cols, dtype=jnp.int32)
    per_irrep = vir_b.shape[0]
    a_orbital = lookup(global_col // per_irrep, vir_a.astype(jnp.float32)).astype(jnp.int32)
    b_orbital = lookup(global_col % per_irrep, vir_b.astype(jnp.float32)).astype(jnp.int32)
    column_energy = lookup(a_orbital, eps_vir) + lookup(b_orbital, eps_vir)
    row_energy = lookup(occ_pairs[0], eps_occ) + lookup(occ_pairs[1], eps_occ)
    denominator = column_energy[None, :] - row_energy[:, None]
    return (other_terms + ladder) / denominator


def solution(mesh):
    in_specs = (
        P("occ", "vir"),
        P("vir", "occ"),
        P("occ", "vir"),
        P(None, "occ"),
        P(),
        P(),
        P(),
        P(),
    )
    out_specs = P("occ", "vir")
    return jax.shard_map(
        per_device, mesh=mesh, in_specs=in_specs, out_specs=out_specs, check_vma=False
    )
```

```python
import jax
import jax.numpy as jnp
from jax import lax
from jax.experimental import pallas as pl
from jax.experimental.pallas import tpu as pltpu
from jax.sharding import PartitionSpec as P

AXES = ("occ", "vir")
NX, NYH, NZ, NYL, NC = 4, 2, 8, 2, 2
SCALE_CHIP = 32.0
SCALE_PAIR = 16.0


def device_id(x, yh, z, yl, c):
    return ((x % NX) * NYH + yh % NYH) * (NZ * NYL * NC) + ((z % NZ) * NYL + yl % NYL) * NC + c % NC


def everywhere():
    return [
        (x, yh, z, yl, c)
        for x in range(NX)
        for yh in range(NYH)
        for z in range(NZ)
        for yl in range(NYL)
        for c in range(NC)
    ]


def moved(target):
    return [(device_id(*spot), device_id(*target(*spot))) for spot in everywhere()]


X_UP = moved(lambda x, yh, z, yl, c: (x + 1, yh, z, yl, c))
X_DOWN = moved(lambda x, yh, z, yl, c: (x - 1, yh, z, yl, c))
Y_FAR = moved(lambda x, yh, z, yl, c: (x, yh + 1, z, yl, c))
CORE = moved(lambda x, yh, z, yl, c: (x, yh, z, yl, c + 1))
Y_NEAR = moved(lambda x, yh, z, yl, c: (x, yh, z, yl + 1, c))


Z_GROUPS = [
    [device_id(x, yh, z, yl, c) for z in range(NZ)]
    for x in range(NX)
    for yh in range(NYH)
    for yl in range(NYL)
    for c in range(NC)
]


def send(block, route):
    return lax.ppermute(block, AXES, route)


def over_z(pieces):
    return lax.all_to_all(pieces, AXES, 0, 0, axis_index_groups=Z_GROUPS, tiled=True)


def lookup(indices, table):
    positions = jnp.arange(table.shape[0], dtype=jnp.int32)
    return jnp.sum(jnp.where(indices[:, None] == positions[None, :], table[None, :], 0.0), axis=1)


def products(rows, cols, plan):
    where = [(i, u) for i, pair in enumerate(rows) for u in range(pair[0].shape[0] // 256)]
    row_arrays = [half for pair in rows for half in pair]
    col_arrays = [chunk for pair in cols for chunk in pair]
    n_rows, depth = len(row_arrays), rows[0][0].shape[1]

    def kernel(*refs):
        row_refs, col_refs, out_ref = refs[:n_rows], refs[n_rows:-1], refs[-1]
        for at, (unit, pair) in enumerate(plan):
            array, block = where[unit]
            total = None
            for half in range(2):
                joined = jnp.concatenate(
                    [col_refs[2 * pair + j][pl.ds(half * depth, depth), :] for j in range(2)], axis=1
                )
                left = row_refs[2 * array + half][pl.ds(256 * block, 256), :]
                term = jnp.dot(left, joined, preferred_element_type=jnp.float32)
                total = term if total is None else total + term
            out_ref[:, pl.ds(32 * at, 32), :] = total.reshape(NZ, 32, 256)

    in_vmem = pl.BlockSpec(memory_space=pltpu.VMEM)
    return pl.pallas_call(
        kernel,
        out_shape=jax.ShapeDtypeStruct((NZ, 32 * len(plan), 256), jnp.float32),
        in_specs=[in_vmem] * (n_rows + len(col_arrays)),
        out_specs=in_vmem,
        compiler_params=pltpu.CompilerParams(vmem_limit_bytes=16 * 1024 * 1024),
        cost_estimate=pl.CostEstimate(flops=1, bytes_accessed=1, transcendentals=0),
    )(*[pltpu.with_memory_space_constraint(array, pltpu.VMEM) for array in row_arrays + col_arrays])


def half_precision(block, scale):
    return (block * scale).astype(jnp.float16)


def reduce_z(batch, scale):
    return jnp.sum(over_z(batch).astype(jnp.float32), axis=0) * (1.0 / scale)


def slots_of(places, early, late, early_far, late_far):
    def kernel(places_ref, early_ref, late_ref, early_far_ref, late_far_ref, out_ref):
        for q in range(4):
            own, at = (early_ref, 96 * q) if q < 3 else (late_ref, 0)
            out_ref[places_ref[2 * q]] = own[pl.ds(at, 96), :]
            place = places_ref[2 * q + 1]
            for unit in range(3):
                ref, order = (
                    (early_far_ref, EARLY_FAR) if (3 + unit, q) in EARLY_FAR else (late_far_ref, LATE_FAR)
                )
                at = 32 * order.index((3 + unit, q))
                out_ref[place, pl.ds(32 * unit, 32), :] = ref[pl.ds(at, 32), :]

    in_vmem = pl.BlockSpec(memory_space=pltpu.VMEM)
    return pl.pallas_call(
        kernel,
        out_shape=jax.ShapeDtypeStruct((NZ, 96, 128), jnp.float32),
        in_specs=[pl.BlockSpec(memory_space=pltpu.SMEM)] + [in_vmem] * 4,
        out_specs=in_vmem,
    )(places, early, late, early_far, late_far)


PLAN = [
    [(u, 0) for u in range(3)],
    [(u, 1) for u in range(3)] + [(3, 0), (3, 1)],
    [(u, 2) for u in range(4)] + [(4, q) for q in range(3)],
    [(u, 3) for u in range(5)],
    [(5, q) for q in range(4)],
]
EARLY_FAR = PLAN[1][3:] + PLAN[2][3:]
LATE_FAR = PLAN[3][3:] + PLAN[4]


def per_device(amplitudes, integrals, other_terms, occ_pairs, vir_a, vir_b, eps_occ, eps_vir):
    vir = lax.axis_index("vir")
    core = vir % NC
    y_low = (vir // NC) % NYL
    barrier = lax.optimization_barrier

    def columns(which, of_core):
        return lax.dynamic_slice_in_dim(integrals, which * 256 + of_core * 128, 128, axis=1)

    x, y_high = lax.axis_index("occ") // NYH, lax.axis_index("occ") % NYH
    shifts = [0, 3 - 2 * y_low, 2, 1 + 2 * y_low]
    places = jnp.stack(
        [2 * ((x + shift) % NX) + (y_high + far) % NYH for shift in shifts for far in range(2)]
    ).astype(jnp.int32)

    def mine(block):
        return lax.dynamic_slice_in_dim(block, y_low * 128, 128, axis=block.ndim - 1)

    def neighbours(block):
        return lax.dynamic_slice_in_dim(block, (1 - y_low) * 128, 128, axis=block.ndim - 1)

    b = tuple(
        jnp.concatenate([columns(j, core), send(columns(j, 1 - core), CORE)], axis=0) for j in range(2)
    )
    p1, m1, ay0 = send(b[0], X_UP), send(b[1], X_DOWN), send(amplitudes[:256], Y_FAR)
    rows = [(amplitudes, send(amplitudes, CORE))]
    cols = [b]
    in0 = half_precision(products(rows, cols, PLAN[0]), SCALE_CHIP)
    s0 = reduce_z(in0, SCALE_CHIP)
    p1, m1, ay0, later, in0 = barrier((p1, m1, ay0, amplitudes, in0))
    p2, m2, ay1 = send(p1, X_UP), send(m1, X_DOWN), send(later[256:512], Y_FAR)
    far = send(ay0, CORE)
    rows, cols = rows + [(ay0, far)], cols + [(p1, m1)]
    new, s0 = barrier((products(rows, cols, PLAN[1]), s0))
    in1 = half_precision(new, SCALE_CHIP)
    s1 = reduce_z(in1, SCALE_CHIP)
    p2, m2, ay1, later, b0, b1, in1 = barrier((p2, m2, ay1, amplitudes, b[0], b[1], in1))
    p3, m3, ay2 = send(b1, X_UP), send(b0, X_DOWN), send(later[512:], Y_FAR)
    far = send(ay1, CORE)
    rows, cols = rows + [(ay1, far)], cols + [(p2, m2)]
    new, s1 = barrier((products(rows, cols, PLAN[2]), s1))
    in2 = half_precision(new, SCALE_CHIP)
    s2 = reduce_z(in2, SCALE_CHIP)
    p3, m3, ay2, in2 = barrier((p3, m3, ay2, in2))
    cols = cols + [(m3, p3)]
    last = [
        products(rows, cols[3:], [(u, 0) for u, _ in PLAN[3]]),
        products([(ay2, send(ay2, CORE))], cols, [(0, q) for _, q in PLAN[4]]),
    ]
    last[1], s2 = barrier((last[1], s2))
    met = [send(half_precision(neighbours(part), SCALE_CHIP), Y_NEAR) for part in last]
    pair = [
        half_precision(mine(part) + got.astype(jnp.float32) * (1.0 / SCALE_CHIP), SCALE_PAIR)
        for part, got in zip(last, met)
    ]
    late = reduce_z(jnp.concatenate(pair, axis=1), SCALE_PAIR)
    early = jnp.concatenate([s0, s1[:96], s2[:96], s1[96:], s2[96:]], axis=0)
    early = mine(early) + send(neighbours(early), Y_NEAR)
    early_far, late_far = send(early[288:], Y_FAR), send(late[96:], Y_FAR)
    ladder = over_z(slots_of(places, early, late, early_far, late_far))
    ladder = ladder.reshape(NZ, 3, 32, 128).transpose(1, 0, 2, 3).reshape(768, 128)

    local_cols = other_terms.shape[1]
    global_col = vir * local_cols + jnp.arange(local_cols, dtype=jnp.int32)
    per_irrep = vir_b.shape[0]
    a_orbital = lookup(global_col // per_irrep, vir_a.astype(jnp.float32)).astype(jnp.int32)
    b_orbital = lookup(global_col % per_irrep, vir_b.astype(jnp.float32)).astype(jnp.int32)
    column_energy = lookup(a_orbital, eps_vir) + lookup(b_orbital, eps_vir)
    row_energy = lookup(occ_pairs[0], eps_occ) + lookup(occ_pairs[1], eps_occ)
    denominator = column_energy[None, :] - row_energy[:, None]
    return (other_terms + ladder) / denominator


def solution(mesh):
    in_specs = (
        P("occ", "vir"),
        P("vir", "occ"),
        P("occ", "vir"),
        P(None, "occ"),
        P(),
        P(),
        P(),
        P(),
    )
    out_specs = P("occ", "vir")
    return jax.shard_map(
        per_device, mesh=mesh, in_specs=in_specs, out_specs=out_specs, check_vma=False
    )
```

```python
import jax
import jax.numpy as jnp
from jax import lax
from jax.experimental import pallas as pl
from jax.experimental.pallas import tpu as pltpu
from jax.sharding import PartitionSpec as P

AXES = ("occ", "vir")
NX, NYH, NZ, NYL, NC = 4, 2, 8, 2, 2
SCALE_CHIP = 32.0
SCALE_PAIR = 16.0


def device_id(x, yh, z, yl, c):
    return ((x % NX) * NYH + yh % NYH) * (NZ * NYL * NC) + ((z % NZ) * NYL + yl % NYL) * NC + c % NC


def everywhere():
    return [
        (x, yh, z, yl, c)
        for x in range(NX)
        for yh in range(NYH)
        for z in range(NZ)
        for yl in range(NYL)
        for c in range(NC)
    ]


def moved(target):
    return [(device_id(*spot), device_id(*target(*spot))) for spot in everywhere()]


X_UP = moved(lambda x, yh, z, yl, c: (x + 1, yh, z, yl, c))
X_DOWN = moved(lambda x, yh, z, yl, c: (x - 1, yh, z, yl, c))
Y_FAR = moved(lambda x, yh, z, yl, c: (x, yh + 1, z, yl, c))
CORE = moved(lambda x, yh, z, yl, c: (x, yh, z, yl, c + 1))
Y_NEAR = moved(lambda x, yh, z, yl, c: (x, yh, z, yl + 1, c))


Z_GROUPS = [
    [device_id(x, yh, z, yl, c) for z in range(NZ)]
    for x in range(NX)
    for yh in range(NYH)
    for yl in range(NYL)
    for c in range(NC)
]


def send(block, route):
    return lax.ppermute(block, AXES, route)


def over_z(pieces):
    return lax.all_to_all(pieces, AXES, 0, 0, axis_index_groups=Z_GROUPS, tiled=True)


def lookup(indices, table):
    positions = jnp.arange(table.shape[0], dtype=jnp.int32)
    return jnp.sum(jnp.where(indices[:, None] == positions[None, :], table[None, :], 0.0), axis=1)


def products(rows, cols, plan):
    where = [(i, u) for i, pair in enumerate(rows) for u in range(pair[0].shape[0] // 256)]
    row_arrays = [half for pair in rows for half in pair]
    col_arrays = [chunk for pair in cols for chunk in pair]
    n_rows, depth = len(row_arrays), rows[0][0].shape[1]

    def kernel(*refs):
        row_refs, col_refs, out_ref = refs[:n_rows], refs[n_rows:-1], refs[-1]
        for at, (unit, pair) in enumerate(plan):
            array, block = where[unit]
            total = None
            for half in range(2):
                joined = jnp.concatenate(
                    [col_refs[2 * pair + j][pl.ds(half * depth, depth), :] for j in range(2)], axis=1
                )
                left = row_refs[2 * array + half][pl.ds(256 * block, 256), :]
                term = jnp.dot(left, joined, preferred_element_type=jnp.float32)
                total = term if total is None else total + term
            out_ref[:, pl.ds(32 * at, 32), :] = total.reshape(NZ, 32, 256)

    in_vmem = pl.BlockSpec(memory_space=pltpu.VMEM)
    return pl.pallas_call(
        kernel,
        out_shape=jax.ShapeDtypeStruct((NZ, 32 * len(plan), 256), jnp.float32),
        in_specs=[in_vmem] * (n_rows + len(col_arrays)),
        out_specs=in_vmem,
        compiler_params=pltpu.CompilerParams(vmem_limit_bytes=16 * 1024 * 1024),
        cost_estimate=pl.CostEstimate(flops=1, bytes_accessed=1, transcendentals=0),
    )(*[pltpu.with_memory_space_constraint(array, pltpu.VMEM) for array in row_arrays + col_arrays])


def half_precision(block, scale):
    return (block * scale).astype(jnp.float16)


def reduce_z(batch, scale):
    return jnp.sum(over_z(batch).astype(jnp.float32), axis=0) * (1.0 / scale)


def slots_of(places, early, late, early_far, late_far):
    def kernel(places_ref, early_ref, late_ref, early_far_ref, late_far_ref, out_ref):
        for q in range(4):
            own, at = (early_ref, 96 * q) if q < 3 else (late_ref, 0)
            out_ref[places_ref[2 * q]] = own[pl.ds(at, 96), :]
            place = places_ref[2 * q + 1]
            for unit in range(3):
                ref, order = (
                    (early_far_ref, EARLY_FAR) if (3 + unit, q) in EARLY_FAR else (late_far_ref, LATE_FAR)
                )
                at = 32 * order.index((3 + unit, q))
                out_ref[place, pl.ds(32 * unit, 32), :] = ref[pl.ds(at, 32), :]

    in_vmem = pl.BlockSpec(memory_space=pltpu.VMEM)
    return pl.pallas_call(
        kernel,
        out_shape=jax.ShapeDtypeStruct((NZ, 96, 128), jnp.float32),
        in_specs=[pl.BlockSpec(memory_space=pltpu.SMEM)] + [in_vmem] * 4,
        out_specs=in_vmem,
    )(places, early, late, early_far, late_far)


PLAN = [
    [(u, 0) for u in range(3)],
    [(u, 1) for u in range(3)] + [(3, 0), (3, 1)],
    [(u, 2) for u in range(4)] + [(4, q) for q in range(3)],
    [(u, 3) for u in range(5)],
    [(5, q) for q in range(4)],
]
EARLY_FAR = PLAN[1][3:] + PLAN[2][3:]
LATE_FAR = PLAN[3][3:] + PLAN[4]


def per_device(amplitudes, integrals, other_terms, occ_pairs, vir_a, vir_b, eps_occ, eps_vir):
    vir = lax.axis_index("vir")
    core = vir % NC
    y_low = (vir // NC) % NYL
    barrier = lax.optimization_barrier

    def columns(which, of_core):
        return lax.dynamic_slice_in_dim(integrals, which * 256 + of_core * 128, 128, axis=1)

    x, y_high = lax.axis_index("occ") // NYH, lax.axis_index("occ") % NYH
    shifts = [0, 3 - 2 * y_low, 1 + 2 * y_low, 2]
    places = jnp.stack(
        [2 * ((x + shift) % NX) + (y_high + far) % NYH for shift in shifts for far in range(2)]
    ).astype(jnp.int32)

    def mine(block):
        return lax.dynamic_slice_in_dim(block, y_low * 128, 128, axis=block.ndim - 1)

    def neighbours(block):
        return lax.dynamic_slice_in_dim(block, (1 - y_low) * 128, 128, axis=block.ndim - 1)

    b = tuple(
        jnp.concatenate([columns(j, core), send(columns(j, 1 - core), CORE)], axis=0) for j in range(2)
    )
    p1, m1, ay0 = send(b[0], X_UP), send(b[1], X_DOWN), send(amplitudes[:256], Y_FAR)
    rows = [(amplitudes, send(amplitudes, CORE))]
    cols = [b]
    in0 = half_precision(products(rows, cols, PLAN[0]), SCALE_CHIP)
    s0 = reduce_z(in0, SCALE_CHIP)
    later, in0 = barrier((amplitudes, in0))
    a1, a2 = later[256:512], later[512:]
    ay0, a1, b0, b1, in0 = barrier((ay0, a1, b[0], b[1], in0))
    p2, m2, ay1 = send(b1, X_UP), send(b0, X_DOWN), send(a1, Y_FAR)
    rows, cols = rows + [(ay0, send(ay0, CORE))], cols + [(p1, m1)]
    new, s0 = barrier((products(rows, cols, PLAN[1]), s0))
    in1 = half_precision(new, SCALE_CHIP)
    s1 = reduce_z(in1, SCALE_CHIP)
    p2, m2, ay1, a2, p1, m1, in1 = barrier((p2, m2, ay1, a2, p1, m1, in1))
    p3, m3, ay2 = send(p1, X_UP), send(m1, X_DOWN), send(a2, Y_FAR)
    rows, cols = rows + [(ay1, send(ay1, CORE))], cols + [(m2, p2)]
    new, s1 = barrier((products(rows, cols, PLAN[2]), s1))
    in2 = half_precision(new, SCALE_CHIP)
    s2 = reduce_z(in2, SCALE_CHIP)
    p3, m3, ay2, in2 = barrier((p3, m3, ay2, in2))
    cols = cols + [(p3, m3)]
    last = [
        products(rows, cols[3:], [(u, 0) for u, _ in PLAN[3]]),
        products([(ay2, send(ay2, CORE))], cols, [(0, q) for _, q in PLAN[4]]),
    ]
    last[1], s2 = barrier((last[1], s2))
    met = [send(half_precision(neighbours(part), SCALE_CHIP), Y_NEAR) for part in last]
    pair = [
        half_precision(mine(part) + got.astype(jnp.float32) * (1.0 / SCALE_CHIP), SCALE_PAIR)
        for part, got in zip(last, met)
    ]
    late = reduce_z(jnp.concatenate(pair, axis=1), SCALE_PAIR)
    early = jnp.concatenate([s0, s1[:96], s2[:96], s1[96:], s2[96:]], axis=0)
    early = mine(early) + send(neighbours(early), Y_NEAR)
    early_far, late_far = send(early[288:], Y_FAR), send(late[96:], Y_FAR)
    ladder = over_z(slots_of(places, early, late, early_far, late_far))
    ladder = ladder.reshape(NZ, 3, 32, 128).transpose(1, 0, 2, 3).reshape(768, 128)

    local_cols = other_terms.shape[1]
    global_col = vir * local_cols + jnp.arange(local_cols, dtype=jnp.int32)
    per_irrep = vir_b.shape[0]
    a_orbital = lookup(global_col // per_irrep, vir_a.astype(jnp.float32)).astype(jnp.int32)
    b_orbital = lookup(global_col % per_irrep, vir_b.astype(jnp.float32)).astype(jnp.int32)
    column_energy = lookup(a_orbital, eps_vir) + lookup(b_orbital, eps_vir)
    row_energy = lookup(occ_pairs[0], eps_occ) + lookup(occ_pairs[1], eps_occ)
    denominator = column_energy[None, :] - row_energy[:, None]
    return (other_terms + ladder) / denominator


def solution(mesh):
    in_specs = (
        P("occ", "vir"),
        P("vir", "occ"),
        P("occ", "vir"),
        P(None, "occ"),
        P(),
        P(),
        P(),
        P(),
    )
    out_specs = P("occ", "vir")
    return jax.shard_map(
        per_device, mesh=mesh, in_specs=in_specs, out_specs=out_specs, check_vma=False
    )
```

```python
import jax
import jax.numpy as jnp
from jax import lax
from jax.experimental import pallas as pl
from jax.experimental.pallas import tpu as pltpu
from jax.sharding import PartitionSpec as P

AXES = ("occ", "vir")
NX, NYH, NZ, NYL, NC = 4, 2, 8, 2, 2
SCALE_CHIP = 32.0
SCALE_PAIR = 16.0


def device_id(x, yh, z, yl, c):
    return ((x % NX) * NYH + yh % NYH) * (NZ * NYL * NC) + ((z % NZ) * NYL + yl % NYL) * NC + c % NC


def everywhere():
    return [
        (x, yh, z, yl, c)
        for x in range(NX)
        for yh in range(NYH)
        for z in range(NZ)
        for yl in range(NYL)
        for c in range(NC)
    ]


def moved(target):
    return [(device_id(*spot), device_id(*target(*spot))) for spot in everywhere()]


X_UP = moved(lambda x, yh, z, yl, c: (x + 1, yh, z, yl, c))
X_DOWN = moved(lambda x, yh, z, yl, c: (x - 1, yh, z, yl, c))
Y_FAR = moved(lambda x, yh, z, yl, c: (x, yh + 1, z, yl, c))
CORE = moved(lambda x, yh, z, yl, c: (x, yh, z, yl, c + 1))
Y_NEAR = moved(lambda x, yh, z, yl, c: (x, yh, z, yl + 1, c))


Z_GROUPS = [
    [device_id(x, yh, z, yl, c) for z in range(NZ)]
    for x in range(NX)
    for yh in range(NYH)
    for yl in range(NYL)
    for c in range(NC)
]


def send(block, route):
    return lax.ppermute(block, AXES, route)


def over_z(pieces):
    return lax.all_to_all(pieces, AXES, 0, 0, axis_index_groups=Z_GROUPS, tiled=True)


def lookup(indices, table):
    positions = jnp.arange(table.shape[0], dtype=jnp.int32)
    return jnp.sum(jnp.where(indices[:, None] == positions[None, :], table[None, :], 0.0), axis=1)


def products(rows, cols, plan):
    where = [(i, u) for i, pair in enumerate(rows) for u in range(pair[0].shape[0] // 256)]
    row_arrays = [half for pair in rows for half in pair]
    col_arrays = [chunk for pair in cols for chunk in pair]
    n_rows, depth = len(row_arrays), rows[0][0].shape[1]

    def kernel(*refs):
        row_refs, col_refs, out_ref = refs[:n_rows], refs[n_rows:-1], refs[-1]
        for at, (unit, pair) in enumerate(plan):
            array, block = where[unit]
            total = None
            for half in range(2):
                joined = jnp.concatenate(
                    [col_refs[2 * pair + j][pl.ds(half * depth, depth), :] for j in range(2)], axis=1
                )
                left = row_refs[2 * array + half][pl.ds(256 * block, 256), :]
                term = jnp.dot(left, joined, preferred_element_type=jnp.float32)
                total = term if total is None else total + term
            out_ref[:, pl.ds(32 * at, 32), :] = total.reshape(NZ, 32, 256)

    in_vmem = pl.BlockSpec(memory_space=pltpu.VMEM)
    return pl.pallas_call(
        kernel,
        out_shape=jax.ShapeDtypeStruct((NZ, 32 * len(plan), 256), jnp.float32),
        in_specs=[in_vmem] * (n_rows + len(col_arrays)),
        out_specs=in_vmem,
        compiler_params=pltpu.CompilerParams(vmem_limit_bytes=16 * 1024 * 1024),
        cost_estimate=pl.CostEstimate(flops=1, bytes_accessed=1, transcendentals=0),
    )(*[pltpu.with_memory_space_constraint(array, pltpu.VMEM) for array in row_arrays + col_arrays])


def half_precision(block, scale):
    return (block * scale).astype(jnp.float16)


def summed(got, scale):
    return jnp.sum(got.astype(jnp.float32), axis=0) * (1.0 / scale)


def reduce_z(batch, scale):
    return summed(over_z(batch), scale)


def slots_of(places, early, late, early_far, late_far):
    def kernel(places_ref, early_ref, late_ref, early_far_ref, late_far_ref, out_ref):
        for q in range(4):
            own, at = (early_ref, 96 * q) if q < 3 else (late_ref, 0)
            out_ref[places_ref[2 * q]] = own[pl.ds(at, 96), :]
            place = places_ref[2 * q + 1]
            for unit in range(3):
                ref, order = (
                    (early_far_ref, EARLY_FAR) if (3 + unit, q) in EARLY_FAR else (late_far_ref, LATE_FAR)
                )
                at = 32 * order.index((3 + unit, q))
                out_ref[place, pl.ds(32 * unit, 32), :] = ref[pl.ds(at, 32), :]

    in_vmem = pl.BlockSpec(memory_space=pltpu.VMEM)
    return pl.pallas_call(
        kernel,
        out_shape=jax.ShapeDtypeStruct((NZ, 96, 128), jnp.float32),
        in_specs=[pl.BlockSpec(memory_space=pltpu.SMEM)] + [in_vmem] * 4,
        out_specs=in_vmem,
    )(places, early, late, early_far, late_far)


PLAN = [
    [(u, 0) for u in range(3)],
    [(u, 1) for u in range(3)] + [(3, 0), (3, 1)],
    [(u, 2) for u in range(4)] + [(4, q) for q in range(3)],
    [(u, 3) for u in range(5)],
    [(5, q) for q in range(4)],
]
EARLY_FAR = PLAN[1][3:] + PLAN[2][3:]
LATE_FAR = PLAN[3][3:] + PLAN[4]


def per_device(amplitudes, integrals, other_terms, occ_pairs, vir_a, vir_b, eps_occ, eps_vir):
    vir = lax.axis_index("vir")
    core = vir % NC
    y_low = (vir // NC) % NYL
    barrier = lax.optimization_barrier

    def columns(which, of_core):
        return lax.dynamic_slice_in_dim(integrals, which * 256 + of_core * 128, 128, axis=1)

    x, y_high = lax.axis_index("occ") // NYH, lax.axis_index("occ") % NYH
    shifts = [0, 3 - 2 * y_low, 1 + 2 * y_low, 2]
    places = jnp.stack(
        [2 * ((x + shift) % NX) + (y_high + far) % NYH for shift in shifts for far in range(2)]
    ).astype(jnp.int32)

    def mine(block):
        return lax.dynamic_slice_in_dim(block, y_low * 128, 128, axis=block.ndim - 1)

    def neighbours(block):
        return lax.dynamic_slice_in_dim(block, (1 - y_low) * 128, 128, axis=block.ndim - 1)

    b = tuple(
        jnp.concatenate([columns(j, core), send(columns(j, 1 - core), CORE)], axis=0) for j in range(2)
    )
    p1, m1, ay0 = send(b[0], X_UP), send(b[1], X_DOWN), send(amplitudes[:256], Y_FAR)
    rows = [(amplitudes, send(amplitudes, CORE))]
    cols = [b]
    in0 = half_precision(products(rows, cols, PLAN[0]), SCALE_CHIP)
    s0 = reduce_z(in0, SCALE_CHIP)
    later, in0 = barrier((amplitudes, in0))
    a1, a2 = later[256:512], later[512:]
    ay0, a1, b0, b1, in0 = barrier((ay0, a1, b[0], b[1], in0))
    p2, m2, ay1 = send(b1, X_UP), send(b0, X_DOWN), send(a1, Y_FAR)
    rows, cols = rows + [(ay0, send(ay0, CORE))], cols + [(p1, m1)]
    new, s0 = barrier((products(rows, cols, PLAN[1]), s0))
    in1 = half_precision(new, SCALE_CHIP)
    got1 = over_z(in1)
    p2, m2, ay1, a2, p1, m1, in1 = barrier((p2, m2, ay1, a2, p1, m1, in1))
    p3, m3, ay2 = send(p1, X_UP), send(m1, X_DOWN), send(a2, Y_FAR)
    rows, cols = rows + [(ay1, send(ay1, CORE))], cols + [(m2, p2)]
    new, got1 = barrier((products(rows, cols, PLAN[2]), got1))
    in2 = half_precision(new, SCALE_CHIP)
    got2 = over_z(in2)
    p3, m3, ay2, in2 = barrier((p3, m3, ay2, in2))
    cols = cols + [(p3, m3)]
    last = [
        products(rows, cols[3:], [(u, 0) for u, _ in PLAN[3]]),
        products([(ay2, send(ay2, CORE))], cols, [(0, q) for _, q in PLAN[4]]),
    ]
    leaving = [half_precision(neighbours(part), SCALE_CHIP) for part in last]
    met = send(leaving[0], Y_NEAR)
    leaving[1], got2, met = barrier((leaving[1], got2, met))
    met = [met, send(leaving[1], Y_NEAR)]
    pair = [
        half_precision(mine(part) + got.astype(jnp.float32) * (1.0 / SCALE_CHIP), SCALE_PAIR)
        for part, got in zip(last, met)
    ]
    late = reduce_z(jnp.concatenate(pair, axis=1), SCALE_PAIR)
    s1, s2 = summed(got1, SCALE_CHIP), summed(got2, SCALE_CHIP)
    early = jnp.concatenate([s0, s1[:96], s2[:96], s1[96:], s2[96:]], axis=0)
    early = mine(early) + send(neighbours(early), Y_NEAR)
    early_far, late_far = send(early[288:], Y_FAR), send(late[96:], Y_FAR)
    ladder = over_z(slots_of(places, early, late, early_far, late_far))
    ladder = ladder.reshape(NZ, 3, 32, 128).transpose(1, 0, 2, 3).reshape(768, 128)

    local_cols = other_terms.shape[1]
    global_col = vir * local_cols + jnp.arange(local_cols, dtype=jnp.int32)
    per_irrep = vir_b.shape[0]
    a_orbital = lookup(global_col // per_irrep, vir_a.astype(jnp.float32)).astype(jnp.int32)
    b_orbital = lookup(global_col % per_irrep, vir_b.astype(jnp.float32)).astype(jnp.int32)
    column_energy = lookup(a_orbital, eps_vir) + lookup(b_orbital, eps_vir)
    row_energy = lookup(occ_pairs[0], eps_occ) + lookup(occ_pairs[1], eps_occ)
    denominator = column_energy[None, :] - row_energy[:, None]
    return (other_terms + ladder) / denominator


def solution(mesh):
    in_specs = (
        P("occ", "vir"),
        P("vir", "occ"),
        P("occ", "vir"),
        P(None, "occ"),
        P(),
        P(),
        P(),
        P(),
    )
    out_specs = P("occ", "vir")
    return jax.shard_map(
        per_device, mesh=mesh, in_specs=in_specs, out_specs=out_specs, check_vma=False
    )
```

```python
import jax
import jax.numpy as jnp
from jax import lax
from jax.experimental import pallas as pl
from jax.experimental.pallas import tpu as pltpu
from jax.sharding import PartitionSpec as P

AXES = ("occ", "vir")
NX, NYH, NZ, NYL, NC = 4, 2, 8, 2, 2
SCALE_CHIP = 32.0
SCALE_PAIR = 16.0


def device_id(x, yh, z, yl, c):
    return ((x % NX) * NYH + yh % NYH) * (NZ * NYL * NC) + ((z % NZ) * NYL + yl % NYL) * NC + c % NC


def everywhere():
    return [
        (x, yh, z, yl, c)
        for x in range(NX)
        for yh in range(NYH)
        for z in range(NZ)
        for yl in range(NYL)
        for c in range(NC)
    ]


def moved(target):
    return [(device_id(*spot), device_id(*target(*spot))) for spot in everywhere()]


X_UP = moved(lambda x, yh, z, yl, c: (x + 1, yh, z, yl, c))
X_DOWN = moved(lambda x, yh, z, yl, c: (x - 1, yh, z, yl, c))
Y_FAR = moved(lambda x, yh, z, yl, c: (x, yh + 1, z, yl, c))
CORE = moved(lambda x, yh, z, yl, c: (x, yh, z, yl, c + 1))
Y_NEAR = moved(lambda x, yh, z, yl, c: (x, yh, z, yl + 1, c))


Z_GROUPS = [
    [device_id(x, yh, z, yl, c) for z in range(NZ)]
    for x in range(NX)
    for yh in range(NYH)
    for yl in range(NYL)
    for c in range(NC)
]


def send(block, route):
    return lax.ppermute(block, AXES, route)


def over_z(pieces):
    return lax.all_to_all(pieces, AXES, 0, 0, axis_index_groups=Z_GROUPS, tiled=True)


def lookup(indices, table):
    positions = jnp.arange(table.shape[0], dtype=jnp.int32)
    return jnp.sum(jnp.where(indices[:, None] == positions[None, :], table[None, :], 0.0), axis=1)


def products(rows, cols, plan):
    where = [(i, u) for i, pair in enumerate(rows) for u in range(pair[0].shape[0] // 256)]
    row_arrays = [half for pair in rows for half in pair]
    col_arrays = [chunk for pair in cols for chunk in pair]
    n_rows, depth = len(row_arrays), rows[0][0].shape[1]

    def kernel(*refs):
        row_refs, col_refs, out_ref = refs[:n_rows], refs[n_rows:-1], refs[-1]
        for at, (unit, pair) in enumerate(plan):
            array, block = where[unit]
            total = None
            for half in range(2):
                joined = jnp.concatenate(
                    [col_refs[2 * pair + j][pl.ds(half * depth, depth), :] for j in range(2)], axis=1
                )
                left = row_refs[2 * array + half][pl.ds(256 * block, 256), :]
                term = jnp.dot(left, joined, preferred_element_type=jnp.float32)
                total = term if total is None else total + term
            out_ref[:, pl.ds(32 * at, 32), :] = total.reshape(NZ, 32, 256)

    in_vmem = pl.BlockSpec(memory_space=pltpu.VMEM)
    return pl.pallas_call(
        kernel,
        out_shape=jax.ShapeDtypeStruct((NZ, 32 * len(plan), 256), jnp.float32),
        in_specs=[in_vmem] * (n_rows + len(col_arrays)),
        out_specs=in_vmem,
        compiler_params=pltpu.CompilerParams(vmem_limit_bytes=16 * 1024 * 1024),
        cost_estimate=pl.CostEstimate(flops=1, bytes_accessed=1, transcendentals=0),
    )(*[pltpu.with_memory_space_constraint(array, pltpu.VMEM) for array in row_arrays + col_arrays])


def half_precision(block, scale):
    return (block * scale).astype(jnp.float16)


def summed(got, scale):
    return jnp.sum(got.astype(jnp.float32), axis=0) * (1.0 / scale)


def reduce_z(batch, scale):
    return summed(over_z(batch), scale)


def slots_of(places, early, late, early_far, late_far):
    def kernel(places_ref, early_ref, late_ref, early_far_ref, late_far_ref, out_ref):
        for q in range(4):
            own, at = (early_ref, 96 * q) if q < 3 else (late_ref, 0)
            out_ref[places_ref[2 * q]] = own[pl.ds(at, 96), :]
            place = places_ref[2 * q + 1]
            for unit in range(3):
                ref, order = (
                    (early_far_ref, EARLY_FAR) if (3 + unit, q) in EARLY_FAR else (late_far_ref, LATE_FAR)
                )
                at = 32 * order.index((3 + unit, q))
                out_ref[place, pl.ds(32 * unit, 32), :] = ref[pl.ds(at, 32), :]

    in_vmem = pl.BlockSpec(memory_space=pltpu.VMEM)
    return pl.pallas_call(
        kernel,
        out_shape=jax.ShapeDtypeStruct((NZ, 96, 128), jnp.float32),
        in_specs=[pl.BlockSpec(memory_space=pltpu.SMEM)] + [in_vmem] * 4,
        out_specs=in_vmem,
    )(places, early, late, early_far, late_far)


PLAN = [
    [(u, 0) for u in range(3)],
    [(u, 1) for u in range(3)] + [(3, 0), (3, 1)],
    [(u, 2) for u in range(4)] + [(4, q) for q in range(3)],
    [(u, 3) for u in range(5)],
    [(5, q) for q in range(4)],
]
EARLY_FAR = PLAN[1][3:] + PLAN[2][3:]
LATE_FAR = PLAN[3][3:] + PLAN[4]


def per_device(amplitudes, integrals, other_terms, occ_pairs, vir_a, vir_b, eps_occ, eps_vir):
    vir = lax.axis_index("vir")
    core = vir % NC
    y_low = (vir // NC) % NYL
    barrier = lax.optimization_barrier

    def columns(which, of_core):
        return lax.dynamic_slice_in_dim(integrals, which * 256 + of_core * 128, 128, axis=1)

    x, y_high = lax.axis_index("occ") // NYH, lax.axis_index("occ") % NYH
    shifts = [0, 3 - 2 * y_low, 1 + 2 * y_low, 2]
    places = jnp.stack(
        [2 * ((x + shift) % NX) + (y_high + far) % NYH for shift in shifts for far in range(2)]
    ).astype(jnp.int32)

    def mine(block):
        return lax.dynamic_slice_in_dim(block, y_low * 128, 128, axis=block.ndim - 1)

    def neighbours(block):
        return lax.dynamic_slice_in_dim(block, (1 - y_low) * 128, 128, axis=block.ndim - 1)

    b = tuple(
        jnp.concatenate([columns(j, core), send(columns(j, 1 - core), CORE)], axis=0) for j in range(2)
    )
    p1, m1, ay0 = send(b[0], X_UP), send(b[1], X_DOWN), send(amplitudes[:256], Y_FAR)
    rows = [(amplitudes, send(amplitudes, CORE))]
    cols = [b]
    in0 = half_precision(products(rows, cols, PLAN[0]), SCALE_CHIP)
    s0 = reduce_z(in0, SCALE_CHIP)
    later, in0 = barrier((amplitudes, in0))
    a1, a2 = later[256:512], later[512:]
    ay0, a1, b0, b1, in0 = barrier((ay0, a1, b[0], b[1], in0))
    p2, m2, ay1 = send(b1, X_UP), send(b0, X_DOWN), send(a1, Y_FAR)
    rows, cols = rows + [(ay0, send(ay0, CORE))], cols + [(p1, m1)]
    in1 = half_precision(products(rows, cols, PLAN[1]), SCALE_CHIP)
    in1, s0 = barrier((in1, s0))
    got1 = over_z(in1)
    p2, m2, ay1, a2, p1, m1, in1 = barrier((p2, m2, ay1, a2, p1, m1, in1))
    p3, m3, ay2 = send(p1, X_UP), send(m1, X_DOWN), send(a2, Y_FAR)
    rows, cols = rows + [(ay1, send(ay1, CORE))], cols + [(m2, p2)]
    new, got1 = barrier((products(rows, cols, PLAN[2]), got1))
    in2 = half_precision(new, SCALE_CHIP)
    got2 = over_z(in2)
    p3, m3, ay2, in2 = barrier((p3, m3, ay2, in2))
    cols = cols + [(p3, m3)]
    last = [
        products(rows, cols[3:], [(u, 0) for u, _ in PLAN[3]]),
        products([(ay2, send(ay2, CORE))], cols, [(0, q) for _, q in PLAN[4]]),
    ]
    leaving = [half_precision(neighbours(part), SCALE_CHIP) for part in last]
    met = send(leaving[0], Y_NEAR)
    leaving[1], got2, met = barrier((leaving[1], got2, met))
    met = [met, send(leaving[1], Y_NEAR)]
    pair = [
        half_precision(mine(part) + got.astype(jnp.float32) * (1.0 / SCALE_CHIP), SCALE_PAIR)
        for part, got in zip(last, met)
    ]
    late = reduce_z(jnp.concatenate(pair, axis=1), SCALE_PAIR)
    s1, s2 = summed(got1, SCALE_CHIP), summed(got2, SCALE_CHIP)
    early = jnp.concatenate([s0, s1[:96], s2[:96], s1[96:], s2[96:]], axis=0)
    early = mine(early) + send(neighbours(early), Y_NEAR)
    early_far, late_far = send(early[288:], Y_FAR), send(late[96:], Y_FAR)
    ladder = over_z(slots_of(places, early, late, early_far, late_far))
    ladder = ladder.reshape(NZ, 3, 32, 128).transpose(1, 0, 2, 3).reshape(768, 128)

    local_cols = other_terms.shape[1]
    global_col = vir * local_cols + jnp.arange(local_cols, dtype=jnp.int32)
    per_irrep = vir_b.shape[0]
    a_orbital = lookup(global_col // per_irrep, vir_a.astype(jnp.float32)).astype(jnp.int32)
    b_orbital = lookup(global_col % per_irrep, vir_b.astype(jnp.float32)).astype(jnp.int32)
    column_energy = lookup(a_orbital, eps_vir) + lookup(b_orbital, eps_vir)
    row_energy = lookup(occ_pairs[0], eps_occ) + lookup(occ_pairs[1], eps_occ)
    denominator = column_energy[None, :] - row_energy[:, None]
    return (other_terms + ladder) / denominator


def solution(mesh):
    in_specs = (
        P("occ", "vir"),
        P("vir", "occ"),
        P("occ", "vir"),
        P(None, "occ"),
        P(),
        P(),
        P(),
        P(),
    )
    out_specs = P("occ", "vir")
    return jax.shard_map(
        per_device, mesh=mesh, in_specs=in_specs, out_specs=out_specs, check_vma=False
    )
```
